256 devices in a mesh: grp: 8 (over x, core), row: 32 (over y, z).
Axes of the slice: x: 4, y: 4, z: 8, core: 2. Of those that a mesh axis runs over, the one named last changes fastest.
Arguments:
- features: bfloat16 [8192, 8192], P('row', 'grp'), may hold values from -0.0625 to 0.0625
- residual: float32 [8192, 576], P('row'), may hold values from -6 to 6
- precond: float32 [8192, 1024], P('grp'), as said below
Outputs:
- coefs: float32 [8192, 576], P('grp')
- section_resid: float32 [8, 8192, 576], P('grp', 'row')
The draws below stay inside these ranges and needn't reach their ends.
Inputs may be any that keep to these rules, and one draw needn't show every extreme that they name: Each 1024 x 1024 block of precond is symmetric and positive definite.
All inputs are finite; a program needn't handle non-finite values.
Results may differ from the reference program's by a relative error of at most 0.009.
Values may be sent and summed in bfloat16 or wider, within the bound.
A program may use at most 64 MiB of HBM per device.

```python
import jax
import jax.numpy as jnp
from jax import lax

BLK = 1024
TGT = 576
ROWS = 8192
NBLK = 8


def draw_precond(key, part):
    first_key = jax.random.fold_in(jax.random.fold_in(key, 11), 0)
    noise = jax.random.normal(first_key, (NBLK, BLK, BLK), jnp.float32)
    scales = jnp.ones((NBLK, BLK), jnp.float32)
    symmetric = (noise + jnp.swapaxes(noise, 1, 2)) / jnp.sqrt(2.0)
    matrix = jnp.eye(BLK, dtype=jnp.float32)[None] + symmetric * (0.3 / jnp.sqrt(float(BLK)))
    roots = jnp.sqrt(scales)
    matrix = roots[:, :, None] * matrix * roots[:, None, :]
    return matrix.reshape(NBLK * BLK, BLK)


def block_scale(key, dims, cuts, least, largest):
    factor_of = 1.0
    for dim, blocks in cuts:
        heights = jax.random.uniform(jax.random.fold_in(jax.random.fold_in(key, 6), dim), (blocks,), jnp.float32, least / len(cuts), largest / len(cuts))
        factor_of = factor_of * jnp.repeat(jnp.exp(heights), dims[dim] // blocks).reshape((-1,) + (1,) * (len(dims) - 1 - dim))
    return factor_of


def centred(rng, shape, spread, bound, shards=(), kind=jnp.bfloat16):
    level = block_scale(rng, shape, shards, -0.22, 0.18) if shards else 1.0
    result = jax.random.normal(rng, shape, jnp.float32) * spread * level
    return jnp.minimum(jnp.maximum(result, -bound), bound).astype(kind)


def setup_inputs(seed: int = 0) -> dict:
    splits = jax.random.split(jax.random.key(seed), 4)
    features = centred(splits[0], (ROWS, NBLK * BLK), ROWS ** -0.5, 0.0625, ((0, 32), (1, 8)))
    residual = centred(splits[1], (ROWS, TGT), 1.0, 6.0, ((0, 32),), jnp.float32)
    precond = draw_precond(jax.random.fold_in(splits[3], 71), 0)
    return dict(features=features, residual=residual, precond=precond)


def reference(features, residual, precond):
    remaining = residual
    coef_list = []
    resid_list = []
    for block_index in range(NBLK):
        block = features[:, block_index * BLK:(block_index + 1) * BLK]
        block_map = precond[block_index * BLK:(block_index + 1) * BLK]
        rounded = remaining.astype(jnp.bfloat16)
        correlation = lax.dot_general(block, rounded, (((0,), (0,)), ((), ())), preferred_element_type=jnp.float32)
        coefficient = jnp.dot(block_map, correlation, precision=lax.Precision.HIGHEST)
        remaining = remaining - jnp.dot(block, coefficient.astype(jnp.bfloat16), preferred_element_type=jnp.float32)
        coef_list.append(coefficient)
        resid_list.append(remaining)
    return jnp.concatenate(coef_list, axis=0), jnp.stack(resid_list, axis=0)
```

```python
import jax
import jax.numpy as jnp
from jax import lax
from jax.experimental import pallas as pl
from jax.experimental.pallas import tpu as pltpu
from jax.sharding import PartitionSpec as P

MESH = pl.DeviceIdType.MESH
F32 = jnp.float32
BF16 = jnp.bfloat16

BLOCKS = 8
NY, NZ = 4, 8
ROWS = 256
BLK = 1024
TGT = 576
PANEL = TGT // BLOCKS
TILES = 5
WIDE = TILES * 16
LANES = BLK // NZ


def far_first():
    moves = [(dy, dz) for dy in range(NY) for dz in range(NZ) if (dy, dz) != (0, 0)]
    hops = lambda m: min(m[0], NY - m[0]) + min(m[1], NZ - m[1])
    return sorted(moves, key=hops, reverse=True)


def join(tiles):
    return jnp.concatenate(
        [tiles[z].reshape(WIDE, LANES) for z in range(NZ)], axis=1
    )


def sweep_kernel(
    feat_hbm, resid_hbm, prec_hbm, coef_out, sect_out,
    a_all, p_all, prec, resid, resid_t, chain, first, part, take, take_x,
    coef_all, coef_in, chain_in, coef_t, sect_t,
    load_sem, first_send, first_recv, own_send, fwd_send, p_recv, a_recv,
    rs_send, rs_send_x, rs_recv, rs_recv_x, ag_send, ag_send_x, ag_recv, ag_recv_x,
    c_send, c_recv, r_send, r_recv,
):
    g = lax.axis_index("grp")
    r = lax.axis_index("row")
    x, core = g // 2, lax.rem(g, 2)
    y, z = r // NZ, lax.rem(r, NZ)
    twice = y == lax.rem(z, NY)
    my_tile = lax.rem(y - z + 2 * NZ, NY)
    sibling = (2 * x + 1 - core, r)

    def remote(src, dst, send, recv, device):
        return pltpu.make_async_remote_copy(
            src_ref=src, dst_ref=dst, send_sem=send, recv_sem=recv,
            device_id=device, device_id_type=MESH,
        )

    def wait(ref, sem):
        pltpu.make_async_copy(ref, ref, sem).wait()

    loads = [
        pltpu.make_async_copy(resid_hbm, resid, load_sem.at[0]),
        pltpu.make_async_copy(feat_hbm, a_all.at[g], load_sem.at[1]),
        pltpu.make_async_copy(prec_hbm, prec, load_sem.at[2]),
    ]
    for copy in loads:
        copy.start()

    loads[0].wait()
    for j in range(5):
        low, high = 128 * j, min(128 * j + 128, TGT)
        resid_t[low:high, :] = resid[:, low:high].T
    resid_t[TGT:, :] = jnp.zeros((resid_t.shape[0] - TGT, ROWS), F32)
    chain[0] = resid_t[pl.ds(pl.multiple_of(g * PANEL, 8), WIDE), :]

    loads[1].wait()
    loads[2].wait()
    mine = a_all[g]

    def map_rows(j, carry):
        at = pl.ds(pl.multiple_of(j * 256, 256), 256)
        rows = prec[at, :]
        high = rows.astype(BF16)
        low = (rows - high.astype(F32)).astype(BF16)
        dims = (((1,), (1,)), ((), ()))
        out = lax.dot_general(mine, high, dims, preferred_element_type=F32)
        out += lax.dot_general(mine, low, dims, preferred_element_type=F32)
        p_all[g, :, at] = out.astype(BF16)
        return carry

    lax.fori_loop(0, BLK // 256, map_rows, 0)

    def store_part(ref, total):
        for k in range(NZ):
            ref[k] = total[:, k * LANES:(k + 1) * LANES].astype(BF16).reshape(
                TILES, 16, LANES
            )

    @pl.when(g == 0)
    def _():
        for to in (4, 5, 2, 3, 6, 7, 1, 0):
            panel = resid_t[PANEL * to:PANEL * to + WIDE, :].astype(BF16)
            total = jnp.dot(panel, p_all[0], preferred_element_type=F32)
            if to == 0:
                store_part(part.at[0], total)
            else:
                store_part(first.at[to - 1], total)
                remote(
                    first.at[to - 1], part.at[0], first_send, first_recv, (to, r)
                ).start()

    @pl.when(g != 0)
    def _():
        wait(part.at[0], first_recv)

    def own_targets():
        return [
            (lax.rem(g + 4, BLOCKS), r),
            (lax.rem(g + 2, BLOCKS), r),
            (lax.rem(g + 6, BLOCKS), r),
            sibling,
        ]

    def take_block(store, recv, sent, b):
        @pl.when(jnp.logical_and(lax.rem(b, 2) == core, b != g))
        def _():
            wait(store.at[b], recv.at[b])
            remote(store.at[b], store.at[b], sent, recv.at[b], sibling).start()

    def need_block(store, recv, b):
        @pl.when(lax.rem(b, 2) != core)
        def _():
            wait(store.at[b], recv.at[b])

    def wait_eight(sem, b):
        @pl.when(twice)
        def _():
            wait(take.at[b, pl.ds(0, 7)], sem)

        @pl.when(jnp.logical_not(twice))
        def _():
            wait(take.at[b, pl.ds(0, 8)], sem)

    moves = far_first()

    def block_step(b, carry):
        @pl.when(b > 0)
        def _():
            need_block(p_all, p_recv, b)
            total = jnp.dot(
                chain[b].astype(BF16), p_all[b], preferred_element_type=F32
            )
            store_part(part.at[b], total)

        def send_part_x(dz):
            zz = lax.rem(z + dz, NZ)
            yy = lax.rem(zz, NY)
            slot = lax.rem(yy - y + NY, NY) * NZ + dz
            remote(
                part.at[b, zz, 4], take_x.at[b, slot], rs_send_x.at[b],
                rs_recv_x.at[b], (g, yy * NZ + zz),
            ).start()

        for dz in (4, 3, 5, 2, 6, 1, 7):
            send_part_x(dz)

        @pl.when(jnp.logical_not(twice))
        def _():
            send_part_x(0)

        for dy, dz in moves:
            yy, zz = lax.rem(y + dy, NY), lax.rem(z + dz, NZ)
            tile = lax.rem(yy - zz + 2 * NZ, NY)
            remote(
                part.at[b, zz, tile], take.at[b, dy * NZ + dz], rs_send.at[b],
                rs_recv.at[b], (g, yy * NZ + zz),
            ).start()

        @pl.when(b == 0)
        def _():
            @pl.when(g > 0)
            def _():
                for to in own_targets():
                    remote(p_all.at[g], p_all.at[g], own_send.at[0], p_recv.at[g], to).start()

            for to in own_targets():
                remote(a_all.at[g], a_all.at[g], own_send.at[1], a_recv.at[g], to).start()

        take_block(a_all, a_recv, fwd_send.at[1], b)

        wait(take.at[b, pl.ds(1, 31)], rs_recv.at[b])
        total = part[b, z, my_tile].astype(F32)
        total += jnp.sum(take[b, 1:].astype(F32), axis=0)
        coef_all[b, z, my_tile] = total.astype(BF16)

        for dy, dz in moves:
            yy, zz = lax.rem(y + dy, NY), lax.rem(z + dz, NZ)
            remote(
                coef_all.at[b, z, my_tile], coef_all.at[b, z, my_tile],
                ag_send.at[b], ag_recv.at[b], (g, yy * NZ + zz),
            ).start()

        @pl.when(twice)
        def _():
            wait(take_x.at[b, pl.ds(1, 31)], rs_recv_x.at[b])
            more = part[b, z, 4].astype(F32)
            more += jnp.sum(take_x[b, 1:].astype(F32), axis=0)
            coef_all[b, z, 4] = more.astype(BF16)
            for dy, dz in moves:
                yy, zz = lax.rem(y + dy, NY), lax.rem(z + dz, NZ)
                remote(
                    coef_all.at[b, z, 4], coef_all.at[b, z, 4],
                    ag_send_x.at[b], ag_recv_x.at[b], (g, yy * NZ + zz),
                ).start()

        @pl.when(b < BLOCKS - 1)
        def _():
            take_block(p_all, p_recv, fwd_send.at[0], b + 1)

        need_block(a_all, a_recv, b)

        wait(take.at[b, pl.ds(1, 31)], ag_recv.at[b])
        wait_eight(ag_recv_x.at[b], b)

        @pl.when(b != g)
        def _():
            remote(coef_all.at[b], coef_in.at[g], c_send.at[b], c_recv.at[g], (b, r)).start()

        weights = join(coef_all[b])
        change = lax.dot_general(
            weights, a_all[b], (((1,), (1,)), ((), ())), preferred_element_type=F32
        )
        chain[b + 1] = chain[b] - change

        @pl.when(b != g)
        def _():
            remote(chain.at[b + 1], chain_in.at[g], r_send.at[b], r_recv.at[g], (b, r)).start()

        return carry

    lax.fori_loop(0, BLOCKS, block_step, 0)

    coef_in[g] = coef_all[g]
    chain_in[g] = chain[g + 1]
    for of in range(BLOCKS):
        @pl.when(g != of)
        def _():
            wait(coef_in.at[of], c_recv.at[of])

        at = slice(PANEL * of, PANEL * (of + 1))
        coef_t[at, :] = join(coef_in[of])[:PANEL].astype(F32)

    for k in range(NZ):
        at = slice(k * LANES, (k + 1) * LANES)
        coef_out[at, :] = coef_t[:, at].T[:, :TGT]

    for of in range(BLOCKS):
        @pl.when(g != of)
        def _():
            wait(chain_in.at[of], r_recv.at[of])

        sect_t[PANEL * of:PANEL * (of + 1), :] = chain_in[of][:PANEL]

    for k in range(ROWS // LANES):
        at = slice(k * LANES, (k + 1) * LANES)
        sect_out[at, :] = sect_t[:, at].T[:, :TGT]

    @pl.when(g == 0)
    def _():
        wait(first, first_send)

    @pl.when(g > 0)
    def _():
        wait(p_all.at[pl.ds(0, 4)], own_send.at[0])

    wait(a_all.at[pl.ds(0, 4)], own_send.at[1])
    wait(a_all.at[pl.ds(0, 3)], fwd_send.at[1])

    @pl.when(jnp.logical_and(core == 0, x > 0))
    def _():
        wait(p_all.at[pl.ds(0, 2)], fwd_send.at[0])

    @pl.when(jnp.logical_or(core == 1, x == 0))
    def _():
        wait(p_all.at[pl.ds(0, 3)], fwd_send.at[0])

    def drain(b, carry):
        wait(take.at[b, pl.ds(1, 31)], rs_send.at[b])
        wait(take.at[b, pl.ds(1, 31)], ag_send.at[b])
        wait_eight(rs_send_x.at[b], b)

        @pl.when(twice)
        def _():
            wait(take.at[b, pl.ds(1, 31)], ag_send_x.at[b])

        @pl.when(b != g)
        def _():
            wait(coef_all.at[b], c_send.at[b])
            wait(chain.at[b + 1], r_send.at[b])

        return carry

    lax.fori_loop(0, BLOCKS, drain, 0)


def local(features, residual, precond):
    tiles = (NZ, TILES, 16, LANES)
    sem = pltpu.SemaphoreType.DMA
    hbm = pl.BlockSpec(memory_space=pl.ANY)
    vmem = pl.BlockSpec(memory_space=pltpu.VMEM)
    coefs, section = pl.pallas_call(
        sweep_kernel,
        name="block_sweep",
        out_shape=(
            jax.ShapeDtypeStruct((BLK, TGT), F32),
            jax.ShapeDtypeStruct((ROWS, TGT), F32),
        ),
        in_specs=[hbm] * 3,
        out_specs=(vmem, vmem),
        scratch_shapes=[
            pltpu.VMEM((BLOCKS, ROWS, BLK), BF16),
            pltpu.VMEM((BLOCKS, ROWS, BLK), BF16),
            pltpu.VMEM((BLK, BLK), F32),
            pltpu.VMEM((ROWS, TGT), F32),
            pltpu.VMEM((640, ROWS), F32),
            pltpu.VMEM((BLOCKS + 1, WIDE, ROWS), F32),
            pltpu.VMEM((BLOCKS - 1,) + tiles, BF16),
            pltpu.VMEM((BLOCKS,) + tiles, BF16),
            pltpu.VMEM((BLOCKS, 32, 16, LANES), BF16),
            pltpu.VMEM((BLOCKS, 32, 16, LANES), BF16),
            pltpu.VMEM((BLOCKS,) + tiles, BF16),
            pltpu.VMEM((BLOCKS,) + tiles, BF16),
            pltpu.VMEM((BLOCKS, WIDE, ROWS), F32),
            pltpu.VMEM((640, BLK), F32),
            pltpu.VMEM((640, ROWS), F32),
            sem((3,)), sem, sem, sem((2,)), sem((2,)), sem((BLOCKS,)), sem((BLOCKS,)),
        ] + [sem((BLOCKS,))] * 12,
        compiler_params=pltpu.CompilerParams(
            has_side_effects=True, vmem_limit_bytes=48 * 2**20
        ),
        cost_estimate=pl.CostEstimate(
            flops=2 * 10**9, bytes_accessed=8 * 10**6, transcendentals=0
        ),
    )(features, residual, precond)
    return coefs, section[None]


def solution(mesh):
    placed = (P("row", "grp"), P("row", None), P("grp", None))
    return jax.shard_map(
        local,
        mesh=mesh,
        in_specs=placed,
        out_specs=(P("grp", None), P("grp", "row", None)),
        check_vma=False,
    )
```

```python
import jax
import jax.numpy as jnp
from jax import lax
from jax.experimental import pallas as pl
from jax.experimental.pallas import tpu as pltpu
from jax.sharding import PartitionSpec as P

MESH = pl.DeviceIdType.MESH
F32 = jnp.float32
BF16 = jnp.bfloat16

BLOCKS = 8
NY, NZ = 4, 8
ROWS = 256
BLK = 1024
TGT = 576
PANEL = TGT // BLOCKS
TILES = 5
WIDE = TILES * 16
LANES = BLK // NZ
CHUNKS = 4


def far_first():
    moves = [(dy, dz) for dy in range(NY) for dz in range(NZ) if (dy, dz) != (0, 0)]
    hops = lambda m: min(m[0], NY - m[0]) + min(m[1], NZ - m[1])
    return sorted(moves, key=hops, reverse=True)


def join(tiles):
    return jnp.concatenate(
        [tiles[z].reshape(WIDE, LANES) for z in range(NZ)], axis=1
    )


def sweep_kernel(
    feat_hbm, resid_hbm, prec_hbm, coef_out, sect_out,
    a_all, p_all, prec, resid, chain, rounded, first, part, take,
    coef_all, coef_in, chain_in,
    load_sem, first_send, first_recv, own_send, fwd_send, p_recv, a_recv,
    rs_send, rs_recv, ag_send, ag_recv, c_send, c_recv, r_send, r_recv,
):
    g = lax.axis_index("grp")
    r = lax.axis_index("row")
    x, core = g // 2, lax.rem(g, 2)
    y, z = r // NZ, lax.rem(r, NZ)
    twice = y == lax.rem(z, NY)
    my_tile = lax.rem(y - z + 2 * NZ, NY) + 1
    sibling = (2 * x + 1 - core, r)

    def remote(src, dst, send, recv, device):
        return pltpu.make_async_remote_copy(
            src_ref=src, dst_ref=dst, send_sem=send, recv_sem=recv,
            device_id=device, device_id_type=MESH,
        )

    def wait(ref, sem):
        pltpu.make_async_copy(ref, ref, sem).wait()

    chunk = BLK // CHUNKS
    loads = [
        pltpu.make_async_copy(feat_hbm, a_all.at[g], load_sem.at[0]),
        pltpu.make_async_copy(resid_hbm, resid.at[pl.ds(0, TGT)], load_sem.at[1]),
    ] + [
        pltpu.make_async_copy(
            prec_hbm.at[pl.ds(j * chunk, chunk)], prec.at[pl.ds(j * chunk, chunk)],
            load_sem.at[2 + j],
        )
        for j in range(CHUNKS)
    ]
    for copy in loads:
        copy.start()

    barrier = pltpu.get_barrier_semaphore()
    moves = far_first()
    others = [(g, lax.rem(y + dy, NY) * NZ + lax.rem(z + dz, NZ)) for dy, dz in moves]
    others += [(lax.rem(g + d, BLOCKS), r) for d in range(1, BLOCKS)]
    for other in others:
        pl.semaphore_signal(barrier, inc=1, device_id=other, device_id_type=MESH)

    def panel(of):
        low = of * PANEL if isinstance(of, int) else pl.multiple_of(of * PANEL, 8)
        return jnp.concatenate(
            [resid[pl.ds(low + 64, 16), :], resid[pl.ds(low, 64), :]], axis=0
        )

    resid[TGT:, :] = jnp.zeros((resid.shape[0] - TGT, ROWS), F32)
    loads[0].wait()
    loads[1].wait()
    chain[...] = panel(g)
    mine = a_all[g]

    def store_part(ref, total):
        for k in range(total.shape[1] // LANES):
            ref[k] = total[:, k * LANES:(k + 1) * LANES].astype(BF16).reshape(
                TILES, 16, LANES
            )

    for j in range(CHUNKS):
        at = slice(j * chunk, (j + 1) * chunk)
        loads[2 + j].wait()
        rows = prec[at, :]
        high = rows.astype(BF16)
        low = (rows - high.astype(F32)).astype(BF16)
        dims = (((1,), (1,)), ((), ()))
        out = lax.dot_general(mine, high, dims, preferred_element_type=F32)
        out += lax.dot_general(mine, low, dims, preferred_element_type=F32)
        mapped = out.astype(BF16)
        p_all[g, :, at] = mapped
        if j == 0:
            pl.semaphore_wait(barrier, len(others))

        @pl.when(g == 0)
        def _():
            groups = pl.ds(j * chunk // LANES, chunk // LANES)
            for to in (4, 5, 2, 6, 3, 7, 1, 0):
                total = jnp.dot(
                    panel(to).astype(BF16), mapped, preferred_element_type=F32
                )
                if to == 0:
                    store_part(part.at[0, groups], total)
                else:
                    store_part(first.at[to - 1, groups], total)
                    remote(
                        first.at[to - 1, groups], part.at[0, groups],
                        first_send, first_recv, (to, r),
                    ).start()

    @pl.when(g != 0)
    def _():
        wait(part.at[0], first_recv)

    def own_targets():
        return [
            (lax.rem(g + 4, BLOCKS), r),
            (lax.rem(g + 2, BLOCKS), r),
            (lax.rem(g + 6, BLOCKS), r),
            sibling,
        ]

    def take_block(store, recv, sent, b):
        @pl.when(jnp.logical_and(lax.rem(b, 2) == core, b != g))
        def _():
            wait(store.at[b], recv.at[b])
            remote(store.at[b], store.at[b], sent, recv.at[b], sibling).start()

    def need_block(store, recv, b):
        @pl.when(lax.rem(b, 2) != core)
        def _():
            wait(store.at[b], recv.at[b])

    def send_own(store, recv, sent):
        for to in own_targets():
            remote(store.at[g], store.at[g], sent, recv.at[g], to).start()

    @pl.when(g == 0)
    def _():
        send_own(a_all, a_recv, own_send.at[1])

    def wait_each(sem):
        @pl.when(twice)
        def _():
            wait(take.at[0, pl.ds(1, 31)], sem)

        @pl.when(jnp.logical_not(twice))
        def _():
            wait(take.at[0, pl.ds(1, 31), 0], sem)

    def wait_rest(sem):
        @pl.when(twice)
        def _():
            wait(take.at[0, pl.ds(1, 19)], sem)

        @pl.when(jnp.logical_not(twice))
        def _():
            wait(take.at[pl.ds(0, 3), pl.ds(0, 13), 0], sem)

    def block_step(b, carry):
        @pl.when(b > 0)
        def _():
            need_block(p_all, p_recv, b)
            total = jnp.dot(rounded[b], p_all[b], preferred_element_type=F32)
            store_part(part.at[b], total)

        for dy, dz in moves:
            yy, zz = lax.rem(y + dy, NY), lax.rem(z + dz, NZ)
            tile = lax.rem(yy - zz + 2 * NZ, NY) + 1
            to, slot = (g, yy * NZ + zz), dy * NZ + dz

            @pl.when(tile == 1)
            def _():
                pair = pl.ds(0, 2)
                remote(
                    part.at[b, zz, pair], take.at[b, slot, pair], rs_send.at[b],
                    rs_recv.at[b], to,
                ).start()

            @pl.when(tile > 1)
            def _():
                remote(
                    part.at[b, zz, tile], take.at[b, slot, 1], rs_send.at[b],
                    rs_recv.at[b], to,
                ).start()

        @pl.when(jnp.logical_or(g == b + 2, jnp.logical_and(b == 0, g == 1)))
        def _():
            send_own(p_all, p_recv, own_send.at[0])
            send_own(a_all, a_recv, own_send.at[1])

        take_block(a_all, a_recv, fwd_send.at[1], b)

        wait_each(rs_recv.at[b])

        def add_up(tile, slot):
            total = part[b, z, tile].astype(F32)
            total += jnp.sum(take[b, 1:, slot].astype(F32), axis=0)
            coef_all[b, z, tile] = total.astype(BF16)

        def spread(ref):
            for dy, dz in moves:
                yy, zz = lax.rem(y + dy, NY), lax.rem(z + dz, NZ)
                remote(ref, ref, ag_send.at[b], ag_recv.at[b], (g, yy * NZ + zz)).start()

        add_up(my_tile, 1)

        @pl.when(twice)
        def _():
            add_up(0, 0)
            spread(coef_all.at[b, z, pl.ds(0, 2)])

        @pl.when(jnp.logical_not(twice))
        def _():
            spread(coef_all.at[b, z, my_tile])

        @pl.when(b < BLOCKS - 1)
        def _():
            take_block(p_all, p_recv, fwd_send.at[0], b + 1)

        need_block(a_all, a_recv, b)

        wait_rest(ag_recv.at[b])

        @pl.when(b != g)
        def _():
            remote(coef_all.at[b], coef_in.at[g], c_send.at[b], c_recv.at[g], (b, r)).start()

        weights = join(coef_all[b])
        change = lax.dot_general(
            weights, a_all[b], (((1,), (1,)), ((), ())), preferred_element_type=F32
        )
        left = chain[...] - change
        chain[...] = left
        rounded[b + 1] = left.astype(BF16)

        @pl.when(b != g)
        def _():
            remote(rounded.at[b + 1], chain_in.at[g], r_send.at[b], r_recv.at[g], (b, r)).start()

        return carry

    lax.fori_loop(0, BLOCKS, block_step, 0)

    coef_in[g] = coef_all[g]
    chain_in[g] = rounded[g + 1]

    def unpack(out, of, rows):
        rows = rows.astype(F32)
        out[PANEL * of:PANEL * of + 64, :] = rows[16:]
        out[PANEL * of + 64:PANEL * of + 72, :] = rows[:8]

    for of in range(BLOCKS):
        @pl.when(g != of)
        def _():
            wait(coef_in.at[of], c_recv.at[of])

        unpack(coef_out, of, join(coef_in[of]))

    for of in range(BLOCKS):
        @pl.when(g != of)
        def _():
            wait(chain_in.at[of], r_recv.at[of])

        unpack(sect_out, of, chain_in[of])

    @pl.when(g == 0)
    def _():
        wait(first, first_send)

    @pl.when(g > 0)
    def _():
        wait(p_all.at[pl.ds(0, 4)], own_send.at[0])

    wait(a_all.at[pl.ds(0, 4)], own_send.at[1])
    wait(a_all.at[pl.ds(0, 3)], fwd_send.at[1])

    @pl.when(jnp.logical_and(core == 0, x > 0))
    def _():
        wait(p_all.at[pl.ds(0, 2)], fwd_send.at[0])

    @pl.when(jnp.logical_or(core == 1, x == 0))
    def _():
        wait(p_all.at[pl.ds(0, 3)], fwd_send.at[0])

    def drain(b, carry):
        wait_rest(rs_send.at[b])
        wait_each(ag_send.at[b])

        @pl.when(b != g)
        def _():
            wait(coef_all.at[b], c_send.at[b])
            wait(rounded.at[b + 1], r_send.at[b])

        return carry

    lax.fori_loop(0, BLOCKS, drain, 0)


def local(features, residual, precond):
    tiles = (NZ, TILES, 16, LANES)
    sem = pltpu.SemaphoreType.DMA
    hbm = pl.BlockSpec(memory_space=pl.ANY)
    vmem = pl.BlockSpec(memory_space=pltpu.VMEM)
    coefs, section = pl.pallas_call(
        sweep_kernel,
        name="block_sweep",
        out_shape=(
            jax.ShapeDtypeStruct((TGT, BLK), F32),
            jax.ShapeDtypeStruct((TGT, ROWS), F32),
        ),
        in_specs=[hbm] * 3,
        out_specs=(vmem, vmem),
        scratch_shapes=[
            pltpu.VMEM((BLOCKS, ROWS, BLK), BF16),
            pltpu.VMEM((BLOCKS, ROWS, BLK), BF16),
            pltpu.VMEM((BLK, BLK), F32),
            pltpu.VMEM((592, ROWS), F32),
            pltpu.VMEM((WIDE, ROWS), F32),
            pltpu.VMEM((BLOCKS + 1, WIDE, ROWS), BF16),
            pltpu.VMEM((BLOCKS - 1,) + tiles, BF16),
            pltpu.VMEM((BLOCKS,) + tiles, BF16),
            pltpu.VMEM((BLOCKS, 32, 2, 16, LANES), BF16),
            pltpu.VMEM((BLOCKS,) + tiles, BF16),
            pltpu.VMEM((BLOCKS,) + tiles, BF16),
            pltpu.VMEM((BLOCKS, WIDE, ROWS), BF16),
            sem((2 + CHUNKS,)), sem, sem, sem((2,)), sem((2,)),
            sem((BLOCKS,)), sem((BLOCKS,)),
        ] + [sem((BLOCKS,))] * 8,
        compiler_params=pltpu.CompilerParams(
            collective_id=0, has_side_effects=True, vmem_limit_bytes=48 * 2**20
        ),
        cost_estimate=pl.CostEstimate(
            flops=2 * 10**9, bytes_accessed=8 * 10**6, transcendentals=0
        ),
    )(features, residual.T, precond)
    return coefs.T, section.T[None]


def solution(mesh):
    placed = (P("row", "grp"), P("row", None), P("grp", None))
    return jax.shard_map(
        local,
        mesh=mesh,
        in_specs=placed,
        out_specs=(P("grp", None), P("grp", "row", None)),
        check_vma=False,
    )
```

```python
import jax
import jax.numpy as jnp
from jax import lax
from jax.experimental import pallas as pl
from jax.experimental.pallas import tpu as pltpu
from jax.sharding import PartitionSpec as P

MESH = pl.DeviceIdType.MESH
F32 = jnp.float32
BF16 = jnp.bfloat16

BLOCKS = 8
NY, NZ = 4, 8
ROWS = 256
BLK = 1024
TGT = 576
PANEL = TGT // BLOCKS
TILES = 5
WIDE = TILES * 16
LANES = BLK // NZ
CHUNKS = 4


def far_first():
    moves = [(dy, dz) for dy in range(NY) for dz in range(NZ) if (dy, dz) != (0, 0)]
    hops = lambda m: min(m[0], NY - m[0]) + min(m[1], NZ - m[1])
    return sorted(moves, key=hops, reverse=True)


def join(tiles):
    return jnp.concatenate(
        [tiles[z].reshape(WIDE, LANES) for z in range(NZ)], axis=1
    )


def sweep_kernel(
    feat_hbm, resid_hbm, prec_hbm, coef_out, sect_out,
    a_all, p_all, prec, resid, chain, rounded, first, part, take,
    coef_all, coef_in, chain_in,
    load_sem, first_send, first_recv, own_send, fwd_send, p_recv, a_recv,
    rs_send, rs_recv, ag_send, ag_recv, c_send, c_recv, r_send, r_recv,
):
    g = lax.axis_index("grp")
    r = lax.axis_index("row")
    x, core = g // 2, lax.rem(g, 2)
    y, z = r // NZ, lax.rem(r, NZ)
    twice = y == lax.rem(z, NY)
    my_tile = lax.rem(y - z + 2 * NZ, NY) + 1
    sibling = (2 * x + 1 - core, r)

    def remote(src, dst, send, recv, device):
        return pltpu.make_async_remote_copy(
            src_ref=src, dst_ref=dst, send_sem=send, recv_sem=recv,
            device_id=device, device_id_type=MESH,
        )

    def wait(ref, sem):
        pltpu.make_async_copy(ref, ref, sem).wait()

    chunk = BLK // CHUNKS
    loads = [
        pltpu.make_async_copy(feat_hbm, a_all.at[g], load_sem.at[0]),
        pltpu.make_async_copy(resid_hbm, resid.at[pl.ds(0, TGT)], load_sem.at[1]),
    ] + [
        pltpu.make_async_copy(
            prec_hbm.at[pl.ds(j * chunk, chunk)], prec.at[pl.ds(j * chunk, chunk)],
            load_sem.at[2 + j],
        )
        for j in range(CHUNKS)
    ]
    for copy in loads:
        copy.start()

    barrier = pltpu.get_barrier_semaphore()
    moves = far_first()
    others = [(g, lax.rem(y + dy, NY) * NZ + lax.rem(z + dz, NZ)) for dy, dz in moves]
    others += [(lax.rem(g + d, BLOCKS), r) for d in range(1, BLOCKS)]
    for other in others:
        pl.semaphore_signal(barrier, inc=1, device_id=other, device_id_type=MESH)

    def panel(of):
        low = of * PANEL if isinstance(of, int) else pl.multiple_of(of * PANEL, 8)
        return jnp.concatenate(
            [resid[pl.ds(low + 64, 16), :], resid[pl.ds(low, 64), :]], axis=0
        )

    resid[TGT:, :] = jnp.zeros((resid.shape[0] - TGT, ROWS), F32)
    loads[0].wait()
    loads[1].wait()
    chain[...] = panel(g)
    mine = a_all[g]

    def store_part(ref, total):
        for k in range(total.shape[1] // LANES):
            ref[k] = total[:, k * LANES:(k + 1) * LANES].astype(BF16).reshape(
                TILES, 16, LANES
            )

    right, left = lax.rem(g + 2, BLOCKS), lax.rem(g + 6, BLOCKS)

    def send_own(store, recv, sent):
        for to in ((right, r), (left, r), sibling):
            remote(store.at[g], store.at[g], sent, recv.at[g], to).start()

    def same_core(b, distance):
        return jnp.logical_and(
            lax.rem(b, 2) == core, lax.rem(x - b // 2 + 4, 4) == distance
        )

    def pass_on(store, recv, sent, b):
        for distance, onward in ((1, right), (3, left)):
            @pl.when(same_core(b, distance))
            def _():
                wait(store.at[b], recv.at[b])
                half = store.at[b, pl.ds(0 if distance == 1 else ROWS // 2, ROWS // 2)]
                remote(half, half, sent, recv.at[b], (onward, r)).start()
                remote(store.at[b], store.at[b], sent, recv.at[b], sibling).start()

    def pass_across(store, recv, sent, b):
        @pl.when(same_core(b, 2))
        def _():
            wait(store.at[b], recv.at[b])
            remote(store.at[b], store.at[b], sent, recv.at[b], sibling).start()

    def need_block(store, recv, b):
        @pl.when(lax.rem(b, 2) != core)
        def _():
            wait(store.at[b], recv.at[b])

    a_way = (a_all, a_recv, fwd_send.at[1])
    p_way = (p_all, p_recv, fwd_send.at[0])

    for j in range(CHUNKS):
        at = slice(j * chunk, (j + 1) * chunk)
        loads[2 + j].wait()
        rows = prec[at, :]
        high = rows.astype(BF16)
        low = (rows - high.astype(F32)).astype(BF16)
        dims = (((1,), (1,)), ((), ()))
        out = lax.dot_general(mine, high, dims, preferred_element_type=F32)
        out += lax.dot_general(mine, low, dims, preferred_element_type=F32)
        mapped = out.astype(BF16)
        p_all[g, :, at] = mapped
        if j == 0:
            pl.semaphore_wait(barrier, len(others))

            @pl.when(g > 1)
            def _():
                send_own(a_all, a_recv, own_send.at[1])

        @pl.when(g == 0)
        def _():
            groups = pl.ds(j * chunk // LANES, chunk // LANES)
            for to in (4, 5, 2, 6, 3, 7, 1, 0):
                total = jnp.dot(
                    panel(to).astype(BF16), mapped, preferred_element_type=F32
                )
                if to == 0:
                    store_part(part.at[0, groups], total)
                else:
                    store_part(first.at[to - 1, groups], total)
                    remote(
                        first.at[to - 1, groups], part.at[0, groups],
                        first_send, first_recv, (to, r),
                    ).start()

    @pl.when(g > 1)
    def _():
        send_own(p_all, p_recv, own_send.at[0])

    @pl.when(g != 0)
    def _():
        wait(part.at[0], first_recv)

    @pl.when(g == 1)
    def _():
        send_own(p_all, p_recv, own_send.at[0])

    @pl.when(g < 2)
    def _():
        send_own(a_all, a_recv, own_send.at[1])

    def wait_each(sem):
        @pl.when(twice)
        def _():
            wait(take.at[0, pl.ds(1, 31)], sem)

        @pl.when(jnp.logical_not(twice))
        def _():
            wait(take.at[0, pl.ds(1, 31), 0], sem)

    def wait_rest(sem):
        @pl.when(twice)
        def _():
            wait(take.at[0, pl.ds(1, 19)], sem)

        @pl.when(jnp.logical_not(twice))
        def _():
            wait(take.at[pl.ds(0, 3), pl.ds(0, 13), 0], sem)

    def block_step(b, carry):
        @pl.when(b > 0)
        def _():
            need_block(p_all, p_recv, b)
            total = jnp.dot(rounded[b], p_all[b], preferred_element_type=F32)
            store_part(part.at[b], total)

        for dy, dz in moves:
            yy, zz = lax.rem(y + dy, NY), lax.rem(z + dz, NZ)
            tile = lax.rem(yy - zz + 2 * NZ, NY) + 1
            to, slot = (g, yy * NZ + zz), dy * NZ + dz

            @pl.when(tile == 1)
            def _():
                pair = pl.ds(0, 2)
                remote(
                    part.at[b, zz, pair], take.at[b, slot, pair], rs_send.at[b],
                    rs_recv.at[b], to,
                ).start()

            @pl.when(tile > 1)
            def _():
                remote(
                    part.at[b, zz, tile], take.at[b, slot, 1], rs_send.at[b],
                    rs_recv.at[b], to,
                ).start()

        @pl.when(b == 0)
        def _():
            pass_on(*a_way, b)

        @pl.when(b > 0)
        def _():
            pass_across(*a_way, b)

            @pl.when(b < BLOCKS - 1)
            def _():
                pass_on(*p_way, b + 1)

        wait_each(rs_recv.at[b])

        def add_up(tile, slot):
            total = part[b, z, tile].astype(F32)
            total += jnp.sum(take[b, 1:, slot].astype(F32), axis=0)
            coef_all[b, z, tile] = total.astype(BF16)

        def spread(ref):
            for dy, dz in moves:
                yy, zz = lax.rem(y + dy, NY), lax.rem(z + dz, NZ)
                remote(ref, ref, ag_send.at[b], ag_recv.at[b], (g, yy * NZ + zz)).start()

        add_up(my_tile, 1)

        @pl.when(twice)
        def _():
            add_up(0, 0)
            spread(coef_all.at[b, z, pl.ds(0, 2)])

        @pl.when(jnp.logical_not(twice))
        def _():
            spread(coef_all.at[b, z, my_tile])

        @pl.when(b == 0)
        def _():
            pass_across(*a_way, b)
            pass_on(*p_way, b + 1)

        @pl.when(b < BLOCKS - 1)
        def _():
            pass_across(*p_way, b + 1)
            pass_on(*a_way, b + 1)

        need_block(a_all, a_recv, b)

        wait_rest(ag_recv.at[b])

        @pl.when(b != g)
        def _():
            remote(coef_all.at[b], coef_in.at[g], c_send.at[b], c_recv.at[g], (b, r)).start()

        weights = join(coef_all[b])
        change = lax.dot_general(
            weights, a_all[b], (((1,), (1,)), ((), ())), preferred_element_type=F32
        )
        remaining = chain[...] - change
        chain[...] = remaining
        rounded[b + 1] = remaining.astype(BF16)

        @pl.when(b != g)
        def _():
            remote(rounded.at[b + 1], chain_in.at[g], r_send.at[b], r_recv.at[g], (b, r)).start()

        return carry

    lax.fori_loop(0, BLOCKS, block_step, 0)

    coef_in[g] = coef_all[g]
    chain_in[g] = rounded[g + 1]

    def unpack(out, of, rows):
        rows = rows.astype(F32)
        out[PANEL * of:PANEL * of + 64, :] = rows[16:]
        out[PANEL * of + 64:PANEL * of + 72, :] = rows[:8]

    for of in range(BLOCKS):
        @pl.when(g != of)
        def _():
            wait(coef_in.at[of], c_recv.at[of])

        unpack(coef_out, of, join(coef_in[of]))

    for of in range(BLOCKS):
        @pl.when(g != of)
        def _():
            wait(chain_in.at[of], r_recv.at[of])

        unpack(sect_out, of, chain_in[of])

    @pl.when(g == 0)
    def _():
        wait(first, first_send)

    @pl.when(g > 0)
    def _():
        wait(p_all.at[pl.ds(0, 3)], own_send.at[0])

    wait(a_all.at[pl.ds(0, 3)], own_send.at[1])
    wait(a_all.at[pl.ds(0, 4)], fwd_send.at[1])

    @pl.when(jnp.logical_or(core == 1, x == 0))
    def _():
        wait(p_all.at[pl.ds(0, 4)], fwd_send.at[0])

    @pl.when(jnp.logical_and(core == 0, x == 2))
    def _():
        wait(p_all.at[pl.ds(0, 3)], fwd_send.at[0])

    @pl.when(jnp.logical_and(core == 0, lax.rem(x, 2) == 1))
    def _():
        wait(p_all.at[pl.ds(0, 5), pl.ds(0, ROWS // 2)], fwd_send.at[0])

    def drain(b, carry):
        wait_rest(rs_send.at[b])
        wait_each(ag_send.at[b])

        @pl.when(b != g)
        def _():
            wait(coef_all.at[b], c_send.at[b])
            wait(rounded.at[b + 1], r_send.at[b])

        return carry

    lax.fori_loop(0, BLOCKS, drain, 0)


def local(features, residual, precond):
    tiles = (NZ, TILES, 16, LANES)
    sem = pltpu.SemaphoreType.DMA
    hbm = pl.BlockSpec(memory_space=pl.ANY)
    vmem = pl.BlockSpec(memory_space=pltpu.VMEM)
    coefs, section = pl.pallas_call(
        sweep_kernel,
        name="block_sweep",
        out_shape=(
            jax.ShapeDtypeStruct((TGT, BLK), F32),
            jax.ShapeDtypeStruct((TGT, ROWS), F32),
        ),
        in_specs=[hbm] * 3,
        out_specs=(vmem, vmem),
        scratch_shapes=[
            pltpu.VMEM((BLOCKS, ROWS, BLK), BF16),
            pltpu.VMEM((BLOCKS, ROWS, BLK), BF16),
            pltpu.VMEM((BLK, BLK), F32),
            pltpu.VMEM((592, ROWS), F32),
            pltpu.VMEM((WIDE, ROWS), F32),
            pltpu.VMEM((BLOCKS + 1, WIDE, ROWS), BF16),
            pltpu.VMEM((BLOCKS - 1,) + tiles, BF16),
            pltpu.VMEM((BLOCKS,) + tiles, BF16),
            pltpu.VMEM((BLOCKS, 32, 2, 16, LANES), BF16),
            pltpu.VMEM((BLOCKS,) + tiles, BF16),
            pltpu.VMEM((BLOCKS,) + tiles, BF16),
            pltpu.VMEM((BLOCKS, WIDE, ROWS), BF16),
            sem((2 + CHUNKS,)), sem, sem, sem((2,)), sem((2,)),
            sem((BLOCKS,)), sem((BLOCKS,)),
        ] + [sem((BLOCKS,))] * 8,
        compiler_params=pltpu.CompilerParams(
            collective_id=0, has_side_effects=True, vmem_limit_bytes=48 * 2**20
        ),
        cost_estimate=pl.CostEstimate(
            flops=2 * 10**9, bytes_accessed=8 * 10**6, transcendentals=0
        ),
    )(features, residual.T, precond)
    return coefs.T, section.T[None]


def solution(mesh):
    placed = (P("row", "grp"), P("row", None), P("grp", None))
    return jax.shard_map(
        local,
        mesh=mesh,
        in_specs=placed,
        out_specs=(P("grp", None), P("grp", "row", None)),
        check_vma=False,
    )
```

```python
import jax
import jax.numpy as jnp
from jax import lax
from jax.experimental import pallas as pl
from jax.experimental.pallas import tpu as pltpu
from jax.sharding import PartitionSpec as P

MESH = pl.DeviceIdType.MESH
F32 = jnp.float32
BF16 = jnp.bfloat16

BLOCKS = 8
NY, NZ = 4, 8
ROWS = 256
BLK = 1024
TGT = 576
PANEL = TGT // BLOCKS
TILES = 5
WIDE = TILES * 16
LANES = BLK // NZ
CHUNKS = 4

CHAINS = ((0, 3), (3, 2))
TURNS = ({0: 1, 1: 2, 2: 0}, {3: 3, 0: 4})


def far_first():
    moves = [(dy, dz) for dy in range(NY) for dz in range(NZ) if (dy, dz) != (0, 0)]
    hops = lambda m: min(m[0], NY - m[0]) + min(m[1], NZ - m[1])
    return sorted(moves, key=hops, reverse=True)


def join(tiles):
    return jnp.concatenate(
        [tiles[z].reshape(WIDE, LANES) for z in range(NZ)], axis=1
    )


def sweep_kernel(
    feat_hbm, resid_hbm, prec_hbm, coef_out, sect_out,
    a_all, p_all, prec, resid, chain, rounded, first, part, take,
    coef_all, coef_in, chain_in,
    load_sem, first_send, first_recv, own_send, fwd_send, p_recv, a_recv,
    rs_send, rs_recv, ag_send, ag_recv, c_send, c_recv, r_send, r_recv,
):
    g = lax.axis_index("grp")
    r = lax.axis_index("row")
    x, core = g // 2, lax.rem(g, 2)
    y, z = r // NZ, lax.rem(r, NZ)
    my_class = lax.rem(y - z + 2 * NZ, NY)
    sibling = (2 * x + 1 - core, r)

    def remote(src, dst, send, recv, device):
        return pltpu.make_async_remote_copy(
            src_ref=src, dst_ref=dst, send_sem=send, recv_sem=recv,
            device_id=device, device_id_type=MESH,
        )

    def wait(ref, sem):
        pltpu.make_async_copy(ref, ref, sem).wait()

    chunk = BLK // CHUNKS
    loads = [
        pltpu.make_async_copy(feat_hbm, a_all.at[g], load_sem.at[0]),
        pltpu.make_async_copy(resid_hbm, resid.at[pl.ds(0, TGT)], load_sem.at[1]),
    ] + [
        pltpu.make_async_copy(
            prec_hbm.at[pl.ds(j * chunk, chunk)], prec.at[pl.ds(j * chunk, chunk)],
            load_sem.at[2 + j],
        )
        for j in range(CHUNKS)
    ]
    for copy in loads:
        copy.start()

    barrier = pltpu.get_barrier_semaphore()
    moves = far_first()
    others = [(g, lax.rem(y + dy, NY) * NZ + lax.rem(z + dz, NZ)) for dy, dz in moves]
    others += [(lax.rem(g + d, BLOCKS), r) for d in range(1, BLOCKS)]
    for other in others:
        pl.semaphore_signal(barrier, inc=1, device_id=other, device_id_type=MESH)

    def panel(of):
        low = of * PANEL if isinstance(of, int) else pl.multiple_of(of * PANEL, 8)
        return jnp.concatenate(
            [resid[pl.ds(low + 64, 16), :], resid[pl.ds(low, 64), :]], axis=0
        )

    resid[TGT:, :] = jnp.zeros((resid.shape[0] - TGT, ROWS), F32)
    loads[0].wait()
    loads[1].wait()
    chain[...] = panel(g)
    mine = a_all[g]

    def store_part(ref, total):
        for k in range(total.shape[1] // LANES):
            ref[k] = total[:, k * LANES:(k + 1) * LANES].astype(BF16).reshape(
                TILES, 16, LANES
            )

    right, left = lax.rem(g + 2, BLOCKS), lax.rem(g + 6, BLOCKS)

    def send_own(store, recv, sent):
        for to in ((right, r), (left, r), sibling):
            remote(store.at[g], store.at[g], sent, recv.at[g], to).start()

    def same_core(b, distance):
        return jnp.logical_and(
            lax.rem(b, 2) == core, lax.rem(x - b // 2 + 4, 4) == distance
        )

    def pass_on(store, recv, sent, b):
        for distance, onward in ((1, right), (3, left)):
            @pl.when(same_core(b, distance))
            def _():
                wait(store.at[b], recv.at[b])
                half = store.at[b, pl.ds(0 if distance == 1 else ROWS // 2, ROWS // 2)]
                remote(half, half, sent, recv.at[b], (onward, r)).start()
                remote(store.at[b], store.at[b], sent, recv.at[b], sibling).start()

    def pass_across(store, recv, sent, b):
        @pl.when(same_core(b, 2))
        def _():
            wait(store.at[b], recv.at[b])
            remote(store.at[b], store.at[b], sent, recv.at[b], sibling).start()

    def need_block(store, recv, b):
        @pl.when(lax.rem(b, 2) != core)
        def _():
            wait(store.at[b], recv.at[b])

    a_way = (a_all, a_recv, fwd_send.at[1])
    p_way = (p_all, p_recv, fwd_send.at[0])

    for j in range(CHUNKS):
        at = slice(j * chunk, (j + 1) * chunk)
        loads[2 + j].wait()
        rows = prec[at, :]
        high = rows.astype(BF16)
        low = (rows - high.astype(F32)).astype(BF16)
        dims = (((1,), (1,)), ((), ()))
        out = lax.dot_general(mine, high, dims, preferred_element_type=F32)
        out += lax.dot_general(mine, low, dims, preferred_element_type=F32)
        mapped = out.astype(BF16)
        p_all[g, :, at] = mapped
        if j == 0:
            pl.semaphore_wait(barrier, len(others))

            @pl.when(g > 1)
            def _():
                send_own(a_all, a_recv, own_send.at[1])

        @pl.when(g == 0)
        def _():
            groups = pl.ds(j * chunk // LANES, chunk // LANES)
            for to in (4, 5, 2, 6, 3, 7, 1, 0):
                total = jnp.dot(
                    panel(to).astype(BF16), mapped, preferred_element_type=F32
                )
                if to == 0:
                    store_part(part.at[0, groups], total)
                else:
                    store_part(first.at[to - 1, groups], total)
                    remote(
                        first.at[to - 1, groups], part.at[0, groups],
                        first_send, first_recv, (to, r),
                    ).start()

    @pl.when(g > 1)
    def _():
        send_own(p_all, p_recv, own_send.at[0])

    @pl.when(g != 0)
    def _():
        wait(part.at[0], first_recv)

    @pl.when(g == 1)
    def _():
        send_own(p_all, p_recv, own_send.at[0])

    @pl.when(g < 2)
    def _():
        send_own(a_all, a_recv, own_send.at[1])

    def adds_up(ch, which):
        has = which == -1
        for k in TURNS[ch]:
            has = jnp.logical_or(has, which == k)
        return has

    def tile_of(ch, which):
        tile = 0
        for k, t in TURNS[ch].items():
            tile = jnp.where(which == k, t, tile)
        return tile

    def wait_rest(ch, sem):
        count = len(TURNS[ch]) * NZ
        mine = adds_up(ch, my_class)

        @pl.when(mine)
        def _():
            wait(take.at[ch, 0, pl.ds(0, count - 1)], sem)

        @pl.when(jnp.logical_not(mine))
        def _():
            wait(take.at[ch, 0, pl.ds(0, count)], sem)

    def send_part(ch, b):
        for dy, dz in moves:
            yy, zz = lax.rem(y + dy, NY), lax.rem(z + dz, NZ)
            which = lax.rem(my_class + dy - dz + 2 * NZ, NY)

            @pl.when(adds_up(ch, which))
            def _():
                remote(
                    part.at[b, zz, tile_of(ch, which)], take.at[ch, b, dy * NZ + dz],
                    rs_send.at[ch, b], rs_recv.at[ch, b], (g, yy * NZ + zz),
                ).start()

    def add_up(ch, b):
        @pl.when(adds_up(ch, my_class))
        def _():
            wait(take.at[ch, b, pl.ds(1, 31)], rs_recv.at[ch, b])
            tile = tile_of(ch, my_class)
            total = part[b, z, tile].astype(F32)
            total += jnp.sum(take[ch, b, 1:].astype(F32), axis=0)
            coef_all[b, z, tile] = total.astype(BF16)
            ref = coef_all.at[b, z, tile]
            for dy, dz in moves:
                yy, zz = lax.rem(y + dy, NY), lax.rem(z + dz, NZ)
                remote(
                    ref, ref, ag_send.at[ch, b], ag_recv.at[ch, b], (g, yy * NZ + zz)
                ).start()

    def rows_of(ch):
        first, count = CHAINS[ch]
        return slice(16 * first, 16 * (first + count))

    def update(ch, b):
        first, count = CHAINS[ch]
        rows = rows_of(ch)
        weights = jnp.concatenate(
            [
                coef_all[b, k, first:first + count].reshape(16 * count, LANES)
                for k in range(NZ)
            ],
            axis=1,
        )
        change = lax.dot_general(
            weights, a_all[b], (((1,), (1,)), ((), ())), preferred_element_type=F32
        )
        remaining = chain[rows, :] - change
        chain[rows, :] = remaining
        rounded[b + 1, rows, :] = remaining.astype(BF16)
        return remaining.astype(BF16)

    def next_part(ch, b, rows):
        first, count = CHAINS[ch]
        total = jnp.dot(rows, p_all[b], preferred_element_type=F32)
        for k in range(NZ):
            part[b, k, first:first + count] = (
                total[:, k * LANES:(k + 1) * LANES].astype(BF16).reshape(count, 16, LANES)
            )

    for ch in (0, 1):
        send_part(ch, 0)

    def block_step(b, carry):
        @pl.when(b == 0)
        def _():
            pass_on(*a_way, b)

        @pl.when(b > 0)
        def _():
            pass_across(*a_way, b)

            @pl.when(b < BLOCKS - 1)
            def _():
                pass_on(*p_way, b + 1)

        for ch in (0, 1):
            add_up(ch, b)

        @pl.when(b == 0)
        def _():
            pass_across(*a_way, b)
            pass_on(*p_way, b + 1)

        @pl.when(b < BLOCKS - 1)
        def _():
            pass_across(*p_way, b + 1)
            pass_on(*a_way, b + 1)

        need_block(a_all, a_recv, b)

        for ch in (0, 1):
            wait_rest(ch, ag_recv.at[ch, b])
            if ch == 1:
                @pl.when(b != g)
                def _():
                    remote(
                        coef_all.at[b], coef_in.at[g], c_send.at[b], c_recv.at[g], (b, r)
                    ).start()

            rows = update(ch, b)

            @pl.when(b < BLOCKS - 1)
            def _():
                if ch == 0:
                    need_block(p_all, p_recv, b + 1)
                next_part(ch, b + 1, rows)
                send_part(ch, b + 1)

        @pl.when(b != g)
        def _():
            remote(rounded.at[b + 1], chain_in.at[g], r_send.at[b], r_recv.at[g], (b, r)).start()

        return carry

    lax.fori_loop(0, BLOCKS, block_step, 0)

    coef_in[g] = coef_all[g]
    chain_in[g] = rounded[g + 1]

    def unpack(out, of, rows):
        rows = rows.astype(F32)
        out[PANEL * of:PANEL * of + 64, :] = rows[16:]
        out[PANEL * of + 64:PANEL * of + 72, :] = rows[:8]

    for of in range(BLOCKS):
        @pl.when(g != of)
        def _():
            wait(coef_in.at[of], c_recv.at[of])

        unpack(coef_out, of, join(coef_in[of]))

    for of in range(BLOCKS):
        @pl.when(g != of)
        def _():
            wait(chain_in.at[of], r_recv.at[of])

        unpack(sect_out, of, chain_in[of])

    @pl.when(g == 0)
    def _():
        wait(first, first_send)

    @pl.when(g > 0)
    def _():
        wait(p_all.at[pl.ds(0, 3)], own_send.at[0])

    wait(a_all.at[pl.ds(0, 3)], own_send.at[1])
    wait(a_all.at[pl.ds(0, 4)], fwd_send.at[1])

    @pl.when(jnp.logical_or(core == 1, x == 0))
    def _():
        wait(p_all.at[pl.ds(0, 4)], fwd_send.at[0])

    @pl.when(jnp.logical_and(core == 0, x == 2))
    def _():
        wait(p_all.at[pl.ds(0, 3)], fwd_send.at[0])

    @pl.when(jnp.logical_and(core == 0, lax.rem(x, 2) == 1))
    def _():
        wait(p_all.at[pl.ds(0, 5), pl.ds(0, ROWS // 2)], fwd_send.at[0])

    def drain(b, carry):
        for ch in (0, 1):
            wait_rest(ch, rs_send.at[ch, b])

            @pl.when(adds_up(ch, my_class))
            def _():
                wait(take.at[ch, b, pl.ds(1, 31)], ag_send.at[ch, b])

        @pl.when(b != g)
        def _():
            wait(coef_all.at[b], c_send.at[b])
            wait(rounded.at[b + 1], r_send.at[b])

        return carry

    lax.fori_loop(0, BLOCKS, drain, 0)


def local(features, residual, precond):
    tiles = (NZ, TILES, 16, LANES)
    sem = pltpu.SemaphoreType.DMA
    hbm = pl.BlockSpec(memory_space=pl.ANY)
    vmem = pl.BlockSpec(memory_space=pltpu.VMEM)
    coefs, section = pl.pallas_call(
        sweep_kernel,
        name="block_sweep",
        out_shape=(
            jax.ShapeDtypeStruct((TGT, BLK), F32),
            jax.ShapeDtypeStruct((TGT, ROWS), F32),
        ),
        in_specs=[hbm] * 3,
        out_specs=(vmem, vmem),
        scratch_shapes=[
            pltpu.VMEM((BLOCKS, ROWS, BLK), BF16),
            pltpu.VMEM((BLOCKS, ROWS, BLK), BF16),
            pltpu.VMEM((BLK, BLK), F32),
            pltpu.VMEM((592, ROWS), F32),
            pltpu.VMEM((WIDE, ROWS), F32),
            pltpu.VMEM((BLOCKS + 1, WIDE, ROWS), BF16),
            pltpu.VMEM((BLOCKS - 1,) + tiles, BF16),
            pltpu.VMEM((BLOCKS,) + tiles, BF16),
            pltpu.VMEM((2, BLOCKS, 32, 16, LANES), BF16),
            pltpu.VMEM((BLOCKS,) + tiles, BF16),
            pltpu.VMEM((BLOCKS,) + tiles, BF16),
            pltpu.VMEM((BLOCKS, WIDE, ROWS), BF16),
            sem((2 + CHUNKS,)), sem, sem, sem((2,)), sem((2,)),
            sem((BLOCKS,)), sem((BLOCKS,)),
        ] + [sem((2, BLOCKS))] * 4 + [sem((BLOCKS,))] * 4,
        compiler_params=pltpu.CompilerParams(
            collective_id=0, has_side_effects=True, vmem_limit_bytes=48 * 2**20
        ),
        cost_estimate=pl.CostEstimate(
            flops=2 * 10**9, bytes_accessed=8 * 10**6, transcendentals=0
        ),
    )(features, residual.T, precond)
    return coefs.T, section.T[None]


def solution(mesh):
    placed = (P("row", "grp"), P("row", None), P("grp", None))
    return jax.shard_map(
        local,
        mesh=mesh,
        in_specs=placed,
        out_specs=(P("grp", None), P("grp", "row", None)),
        check_vma=False,
    )
```

```python
import jax
import jax.numpy as jnp
from jax import lax
from jax.experimental import pallas as pl
from jax.experimental.pallas import tpu as pltpu
from jax.sharding import PartitionSpec as P

MESH = pl.DeviceIdType.MESH
F32 = jnp.float32
BF16 = jnp.bfloat16

BLOCKS = 8
NY, NZ = 4, 8
ROWS = 256
BLK = 1024
TGT = 576
PANEL = TGT // BLOCKS
TILES = 5
WIDE = TILES * 16
LANES = BLK // NZ
CHUNKS = 4

CHAINS = ((0, 3), (3, 2))
TURNS = ({0: 1, 1: 2, 2: 0}, {3: 3, 0: 4})


def far_first():
    moves = [(dy, dz) for dy in range(NY) for dz in range(NZ) if (dy, dz) != (0, 0)]
    hops = lambda m: min(m[0], NY - m[0]) + min(m[1], NZ - m[1])
    return sorted(moves, key=hops, reverse=True)


def join(tiles):
    return jnp.concatenate(
        [tiles[z].reshape(WIDE, LANES) for z in range(NZ)], axis=1
    )


def sweep_kernel(
    feat_hbm, resid_hbm, prec_hbm, coef_out, sect_out,
    a_all, p_all, prec, resid, chain, rounded, first, part, take,
    coef_all, coef_in, chain_in,
    load_sem, first_send, first_recv, own_send, fwd_send, p_recv, a_recv,
    rs_send, rs_recv, ag_send, ag_recv, c_send, c_recv, r_send, r_recv,
):
    g = lax.axis_index("grp")
    r = lax.axis_index("row")
    x, core = g // 2, lax.rem(g, 2)
    y, z = r // NZ, lax.rem(r, NZ)
    my_class = lax.rem(y - z + 2 * NZ, NY)
    sibling = (2 * x + 1 - core, r)

    def remote(src, dst, send, recv, device):
        return pltpu.make_async_remote_copy(
            src_ref=src, dst_ref=dst, send_sem=send, recv_sem=recv,
            device_id=device, device_id_type=MESH,
        )

    def wait(ref, sem):
        pltpu.make_async_copy(ref, ref, sem).wait()

    chunk = BLK // CHUNKS
    loads = [
        pltpu.make_async_copy(feat_hbm, a_all.at[g], load_sem.at[0]),
        pltpu.make_async_copy(resid_hbm, resid.at[pl.ds(0, TGT)], load_sem.at[1]),
    ] + [
        pltpu.make_async_copy(
            prec_hbm.at[pl.ds(j * chunk, chunk)], prec.at[pl.ds(j * chunk, chunk)],
            load_sem.at[2 + j],
        )
        for j in range(CHUNKS)
    ]
    for copy in loads:
        copy.start()

    barrier = pltpu.get_barrier_semaphore()
    moves = far_first()
    others = [(g, lax.rem(y + dy, NY) * NZ + lax.rem(z + dz, NZ)) for dy, dz in moves]
    others += [(lax.rem(g + d, BLOCKS), r) for d in range(1, BLOCKS)]
    for other in others:
        pl.semaphore_signal(barrier, inc=1, device_id=other, device_id_type=MESH)

    def panel(of):
        low = of * PANEL if isinstance(of, int) else pl.multiple_of(of * PANEL, 8)
        return jnp.concatenate(
            [resid[pl.ds(low + 64, 16), :], resid[pl.ds(low, 64), :]], axis=0
        )

    resid[TGT:, :] = jnp.zeros((resid.shape[0] - TGT, ROWS), F32)
    loads[0].wait()
    loads[1].wait()
    chain[...] = panel(g)
    mine = a_all[g]

    def store_part(ref, total):
        for k in range(total.shape[1] // LANES):
            ref[k] = total[:, k * LANES:(k + 1) * LANES].astype(BF16).reshape(
                TILES, 16, LANES
            )

    right, left = lax.rem(g + 2, BLOCKS), lax.rem(g + 6, BLOCKS)

    def send_own(store, recv, sent):
        for to in ((right, r), (left, r), sibling):
            remote(store.at[g], store.at[g], sent, recv.at[g], to).start()

    def same_core(b, distance):
        return jnp.logical_and(
            lax.rem(b, 2) == core, lax.rem(x - b // 2 + 4, 4) == distance
        )

    def pass_on(store, recv, sent, b):
        for distance, onward in ((1, right), (3, left)):
            @pl.when(same_core(b, distance))
            def _():
                wait(store.at[b], recv.at[b])
                half = store.at[b, pl.ds(0 if distance == 1 else ROWS // 2, ROWS // 2)]
                remote(half, half, sent, recv.at[b], (onward, r)).start()
                remote(store.at[b], store.at[b], sent, recv.at[b], sibling).start()

    def pass_across(store, recv, sent, b):
        @pl.when(same_core(b, 2))
        def _():
            wait(store.at[b], recv.at[b])
            remote(store.at[b], store.at[b], sent, recv.at[b], sibling).start()

    def need_block(store, recv, b):
        @pl.when(lax.rem(b, 2) != core)
        def _():
            wait(store.at[b], recv.at[b])

    a_way = (a_all, a_recv, fwd_send.at[1])
    p_way = (p_all, p_recv, fwd_send.at[0])

    for j in range(CHUNKS):
        at = slice(j * chunk, (j + 1) * chunk)
        loads[2 + j].wait()
        rows = prec[at, :]
        high = rows.astype(BF16)
        low = (rows - high.astype(F32)).astype(BF16)
        dims = (((1,), (1,)), ((), ()))
        out = lax.dot_general(mine, high, dims, preferred_element_type=F32)
        out += lax.dot_general(mine, low, dims, preferred_element_type=F32)
        mapped = out.astype(BF16)
        p_all[g, :, at] = mapped
        if j == 0:
            pl.semaphore_wait(barrier, len(others))

            @pl.when(g > 0)
            def _():
                send_own(a_all, a_recv, own_send.at[1])

        @pl.when(g == 0)
        def _():
            groups = pl.ds(j * chunk // LANES, chunk // LANES)
            for to in (4, 5, 2, 6, 3, 7, 1, 0):
                total = jnp.dot(
                    panel(to).astype(BF16), mapped, preferred_element_type=F32
                )
                if to == 0:
                    store_part(part.at[0, groups], total)
                else:
                    store_part(first.at[to - 1, groups], total)
                    remote(
                        first.at[to - 1, groups], part.at[0, groups],
                        first_send, first_recv, (to, r),
                    ).start()

    @pl.when(g > 1)
    def _():
        send_own(p_all, p_recv, own_send.at[0])

    @pl.when(g != 0)
    def _():
        wait(part.at[0], first_recv)

    @pl.when(g == 1)
    def _():
        send_own(p_all, p_recv, own_send.at[0])

    @pl.when(g == 0)
    def _():
        send_own(a_all, a_recv, own_send.at[1])

    def adds_up(ch, which):
        has = which == -1
        for k in TURNS[ch]:
            has = jnp.logical_or(has, which == k)
        return has

    def tile_of(ch, which):
        tile = 0
        for k, t in TURNS[ch].items():
            tile = jnp.where(which == k, t, tile)
        return tile

    def wait_rest(ch, sem):
        count = len(TURNS[ch]) * NZ
        mine = adds_up(ch, my_class)

        @pl.when(mine)
        def _():
            wait(take.at[ch, 0, pl.ds(0, count - 1)], sem)

        @pl.when(jnp.logical_not(mine))
        def _():
            wait(take.at[ch, 0, pl.ds(0, count)], sem)

    def send_part(ch, b):
        for dy, dz in moves:
            yy, zz = lax.rem(y + dy, NY), lax.rem(z + dz, NZ)
            which = lax.rem(my_class + dy - dz + 2 * NZ, NY)

            @pl.when(adds_up(ch, which))
            def _():
                remote(
                    part.at[b, zz, tile_of(ch, which)], take.at[ch, b, dy * NZ + dz],
                    rs_send.at[ch, b], rs_recv.at[ch, b], (g, yy * NZ + zz),
                ).start()

    def add_up(ch, b):
        @pl.when(adds_up(ch, my_class))
        def _():
            wait(take.at[ch, b, pl.ds(1, 31)], rs_recv.at[ch, b])
            tile = tile_of(ch, my_class)
            total = part[b, z, tile].astype(F32)
            total += jnp.sum(take[ch, b, 1:].astype(F32), axis=0)
            coef_all[b, z, tile] = total.astype(BF16)
            ref = coef_all.at[b, z, tile]
            for dy, dz in moves:
                yy, zz = lax.rem(y + dy, NY), lax.rem(z + dz, NZ)
                remote(
                    ref, ref, ag_send.at[ch, b], ag_recv.at[ch, b], (g, yy * NZ + zz)
                ).start()

    def rows_of(ch):
        first, count = CHAINS[ch]
        return slice(16 * first, 16 * (first + count))

    def update(ch, b):
        first, count = CHAINS[ch]
        rows = rows_of(ch)
        weights = jnp.concatenate(
            [
                coef_all[b, k, first:first + count].reshape(16 * count, LANES)
                for k in range(NZ)
            ],
            axis=1,
        )
        change = lax.dot_general(
            weights, a_all[b], (((1,), (1,)), ((), ())), preferred_element_type=F32
        )
        remaining = chain[rows, :] - change
        chain[rows, :] = remaining
        rounded[b + 1, rows, :] = remaining.astype(BF16)
        return remaining.astype(BF16)

    def next_part(ch, b, rows):
        first, count = CHAINS[ch]
        total = jnp.dot(rows, p_all[b], preferred_element_type=F32)
        for k in range(NZ):
            part[b, k, first:first + count] = (
                total[:, k * LANES:(k + 1) * LANES].astype(BF16).reshape(count, 16, LANES)
            )

    for ch in (0, 1):
        send_part(ch, 0)

    def block_step(b, carry):
        @pl.when(b == 0)
        def _():
            pass_on(*a_way, b)

        @pl.when(b > 0)
        def _():
            pass_across(*a_way, b)

            @pl.when(b < BLOCKS - 1)
            def _():
                pass_on(*p_way, b + 1)

        for ch in (0, 1):
            add_up(ch, b)

        @pl.when(b == 0)
        def _():
            pass_across(*a_way, b)
            pass_on(*p_way, b + 1)

        @pl.when(b < BLOCKS - 1)
        def _():
            pass_across(*p_way, b + 1)
            pass_on(*a_way, b + 1)

        need_block(a_all, a_recv, b)

        for ch in (0, 1):
            wait_rest(ch, ag_recv.at[ch, b])
            if ch == 1:
                @pl.when(b != g)
                def _():
                    remote(
                        coef_all.at[b], coef_in.at[g], c_send.at[b], c_recv.at[g], (b, r)
                    ).start()

            rows = update(ch, b)

            @pl.when(b < BLOCKS - 1)
            def _():
                if ch == 0:
                    need_block(p_all, p_recv, b + 1)
                next_part(ch, b + 1, rows)
                send_part(ch, b + 1)

        @pl.when(b != g)
        def _():
            remote(rounded.at[b + 1], chain_in.at[g], r_send.at[b], r_recv.at[g], (b, r)).start()

        return carry

    lax.fori_loop(0, BLOCKS, block_step, 0)

    coef_in[g] = coef_all[g]
    chain_in[g] = rounded[g + 1]

    def unpack(out, of, rows):
        rows = rows.astype(F32)
        out[PANEL * of:PANEL * of + 64, :] = rows[16:]
        out[PANEL * of + 64:PANEL * of + 72, :] = rows[:8]

    for of in range(BLOCKS):
        @pl.when(g != of)
        def _():
            wait(coef_in.at[of], c_recv.at[of])

        unpack(coef_out, of, join(coef_in[of]))

    for of in range(BLOCKS):
        @pl.when(g != of)
        def _():
            wait(chain_in.at[of], r_recv.at[of])

        unpack(sect_out, of, chain_in[of])

    @pl.when(g == 0)
    def _():
        wait(first, first_send)

    @pl.when(g > 0)
    def _():
        wait(p_all.at[pl.ds(0, 3)], own_send.at[0])

    wait(a_all.at[pl.ds(0, 3)], own_send.at[1])
    wait(a_all.at[pl.ds(0, 4)], fwd_send.at[1])

    @pl.when(jnp.logical_or(core == 1, x == 0))
    def _():
        wait(p_all.at[pl.ds(0, 4)], fwd_send.at[0])

    @pl.when(jnp.logical_and(core == 0, x == 2))
    def _():
        wait(p_all.at[pl.ds(0, 3)], fwd_send.at[0])

    @pl.when(jnp.logical_and(core == 0, lax.rem(x, 2) == 1))
    def _():
        wait(p_all.at[pl.ds(0, 5), pl.ds(0, ROWS // 2)], fwd_send.at[0])

    def drain(b, carry):
        for ch in (0, 1):
            wait_rest(ch, rs_send.at[ch, b])

            @pl.when(adds_up(ch, my_class))
            def _():
                wait(take.at[ch, b, pl.ds(1, 31)], ag_send.at[ch, b])

        @pl.when(b != g)
        def _():
            wait(coef_all.at[b], c_send.at[b])
            wait(rounded.at[b + 1], r_send.at[b])

        return carry

    lax.fori_loop(0, BLOCKS, drain, 0)


def local(features, residual, precond):
    tiles = (NZ, TILES, 16, LANES)
    sem = pltpu.SemaphoreType.DMA
    hbm = pl.BlockSpec(memory_space=pl.ANY)
    vmem = pl.BlockSpec(memory_space=pltpu.VMEM)
    coefs, section = pl.pallas_call(
        sweep_kernel,
        name="block_sweep",
        out_shape=(
            jax.ShapeDtypeStruct((TGT, BLK), F32),
            jax.ShapeDtypeStruct((TGT, ROWS), F32),
        ),
        in_specs=[hbm] * 3,
        out_specs=(vmem, vmem),
        scratch_shapes=[
            pltpu.VMEM((BLOCKS, ROWS, BLK), BF16),
            pltpu.VMEM((BLOCKS, ROWS, BLK), BF16),
            pltpu.VMEM((BLK, BLK), F32),
            pltpu.VMEM((592, ROWS), F32),
            pltpu.VMEM((WIDE, ROWS), F32),
            pltpu.VMEM((BLOCKS + 1, WIDE, ROWS), BF16),
            pltpu.VMEM((BLOCKS - 1,) + tiles, BF16),
            pltpu.VMEM((BLOCKS,) + tiles, BF16),
            pltpu.VMEM((2, BLOCKS, 32, 16, LANES), BF16),
            pltpu.VMEM((BLOCKS,) + tiles, BF16),
            pltpu.VMEM((BLOCKS,) + tiles, BF16),
            pltpu.VMEM((BLOCKS, WIDE, ROWS), BF16),
            sem((2 + CHUNKS,)), sem, sem, sem((2,)), sem((2,)),
            sem((BLOCKS,)), sem((BLOCKS,)),
        ] + [sem((2, BLOCKS))] * 4 + [sem((BLOCKS,))] * 4,
        compiler_params=pltpu.CompilerParams(
            collective_id=0, has_side_effects=True, vmem_limit_bytes=48 * 2**20
        ),
        cost_estimate=pl.CostEstimate(
            flops=2 * 10**9, bytes_accessed=8 * 10**6, transcendentals=0
        ),
    )(features, residual.T, precond)
    return coefs.T, section.T[None]


def solution(mesh):
    placed = (P("row", "grp"), P("row", None), P("grp", None))
    return jax.shard_map(
        local,
        mesh=mesh,
        in_specs=placed,
        out_specs=(P("grp", None), P("grp", "row", None)),
        check_vma=False,
    )
```

```python
import jax
import jax.numpy as jnp
from jax import lax
from jax.experimental import pallas as pl
from jax.experimental.pallas import tpu as pltpu
from jax.sharding import PartitionSpec as P

MESH = pl.DeviceIdType.MESH
F32 = jnp.float32
BF16 = jnp.bfloat16

BLOCKS = 8
NY, NZ = 4, 8
ROWS = 256
BLK = 1024
TGT = 576
PANEL = TGT // BLOCKS
TILES = 5
WIDE = TILES * 16
LANES = BLK // NZ
CHUNKS = 4

CHAINS = ((0, 3), (3, 2))
TURNS = ({0: 1, 1: 2, 2: 0}, {3: 3, 0: 4})


def far_first():
    moves = [(dy, dz) for dy in range(NY) for dz in range(NZ) if (dy, dz) != (0, 0)]
    hops = lambda m: min(m[0], NY - m[0]) + min(m[1], NZ - m[1])
    return sorted(moves, key=hops, reverse=True)


def join(tiles):
    return jnp.concatenate(
        [tiles[z].reshape(WIDE, LANES) for z in range(NZ)], axis=1
    )


def sweep_kernel(
    feat_hbm, resid_hbm, prec_hbm, coef_out, sect_out,
    a_all, p_all, prec, resid, chain, rounded, first, part, take,
    coef_all, coef_in, chain_in, turned,
    load_sem, first_send, first_recv, own_send, fwd_send, p_recv, a_recv,
    rs_send, rs_recv, ag_send, ag_recv, c_send, c_recv, r_send, r_recv,
):
    g = lax.axis_index("grp")
    r = lax.axis_index("row")
    x, core = g // 2, lax.rem(g, 2)
    y, z = r // NZ, lax.rem(r, NZ)
    my_class = lax.rem(y - z + 2 * NZ, NY)
    sibling = (2 * x + 1 - core, r)

    def remote(src, dst, send, recv, device):
        return pltpu.make_async_remote_copy(
            src_ref=src, dst_ref=dst, send_sem=send, recv_sem=recv,
            device_id=device, device_id_type=MESH,
        )

    def wait(ref, sem):
        pltpu.make_async_copy(ref, ref, sem).wait()

    chunk = BLK // CHUNKS
    loads = [
        pltpu.make_async_copy(feat_hbm, a_all.at[g], load_sem.at[0]),
        pltpu.make_async_copy(resid_hbm, resid.at[pl.ds(0, TGT)], load_sem.at[1]),
    ] + [
        pltpu.make_async_copy(
            prec_hbm.at[pl.ds(j * chunk, chunk)], prec.at[pl.ds(j * chunk, chunk)],
            load_sem.at[2 + j],
        )
        for j in range(CHUNKS)
    ]
    for copy in loads:
        copy.start()

    barrier = pltpu.get_barrier_semaphore()
    moves = far_first()
    others = [(g, lax.rem(y + dy, NY) * NZ + lax.rem(z + dz, NZ)) for dy, dz in moves]
    others += [(lax.rem(g + d, BLOCKS), r) for d in range(1, BLOCKS)]
    for other in others:
        pl.semaphore_signal(barrier, inc=1, device_id=other, device_id_type=MESH)

    def panel(of):
        low = of * PANEL if isinstance(of, int) else pl.multiple_of(of * PANEL, 8)
        return jnp.concatenate(
            [resid[pl.ds(low + 64, 16), :], resid[pl.ds(low, 64), :]], axis=0
        )

    resid[TGT:, :] = jnp.zeros((resid.shape[0] - TGT, ROWS), F32)
    loads[0].wait()
    loads[1].wait()
    chain[...] = panel(g)
    mine = a_all[g]

    def store_part(ref, total):
        for k in range(total.shape[1] // LANES):
            ref[k] = total[:, k * LANES:(k + 1) * LANES].astype(BF16).reshape(
                TILES, 16, LANES
            )

    right, left = lax.rem(g + 2, BLOCKS), lax.rem(g + 6, BLOCKS)

    def send_own(store, recv, sent):
        for to in ((right, r), (left, r), sibling):
            remote(store.at[g], store.at[g], sent, recv.at[g], to).start()

    def same_core(b, distance):
        return jnp.logical_and(
            lax.rem(b, 2) == core, lax.rem(x - b // 2 + 4, 4) == distance
        )

    def pass_on(store, recv, sent, b):
        for distance, onward in ((1, right), (3, left)):
            @pl.when(same_core(b, distance))
            def _():
                wait(store.at[b], recv.at[b])
                half = store.at[b, pl.ds(0 if distance == 1 else ROWS // 2, ROWS // 2)]
                remote(half, half, sent, recv.at[b], (onward, r)).start()
                remote(store.at[b], store.at[b], sent, recv.at[b], sibling).start()

    def pass_across(store, recv, sent, b):
        @pl.when(same_core(b, 2))
        def _():
            wait(store.at[b], recv.at[b])
            remote(store.at[b], store.at[b], sent, recv.at[b], sibling).start()

    def need_block(store, recv, b):
        @pl.when(lax.rem(b, 2) != core)
        def _():
            wait(store.at[b], recv.at[b])

    a_way = (a_all, a_recv, fwd_send.at[1])
    p_way = (p_all, p_recv, fwd_send.at[0])

    for j in range(CHUNKS):
        at = slice(j * chunk, (j + 1) * chunk)
        loads[2 + j].wait()
        rows = prec[at, :]
        high = rows.astype(BF16)
        low = (rows - high.astype(F32)).astype(BF16)
        dims = (((1,), (1,)), ((), ()))
        out = lax.dot_general(mine, high, dims, preferred_element_type=F32)
        out += lax.dot_general(mine, low, dims, preferred_element_type=F32)
        mapped = out.astype(BF16)
        p_all[g, :, at] = mapped
        if j == 0:
            pl.semaphore_wait(barrier, len(others))

            @pl.when(g > 0)
            def _():
                send_own(a_all, a_recv, own_send.at[1])

        @pl.when(g == 0)
        def _():
            groups = pl.ds(j * chunk // LANES, chunk // LANES)
            for to in (4, 5, 2, 6, 3, 7, 1, 0):
                total = jnp.dot(
                    panel(to).astype(BF16), mapped, preferred_element_type=F32
                )
                if to == 0:
                    store_part(part.at[0, groups], total)
                else:
                    store_part(first.at[to - 1, groups], total)
                    remote(
                        first.at[to - 1, groups], part.at[0, groups],
                        first_send, first_recv, (to, r),
                    ).start()

    @pl.when(g > 1)
    def _():
        send_own(p_all, p_recv, own_send.at[0])

    @pl.when(g != 0)
    def _():
        wait(part.at[0], first_recv)

    @pl.when(g == 1)
    def _():
        send_own(p_all, p_recv, own_send.at[0])

    @pl.when(g == 0)
    def _():
        send_own(a_all, a_recv, own_send.at[1])

    def adds_up(ch, which):
        has = which == -1
        for k in TURNS[ch]:
            has = jnp.logical_or(has, which == k)
        return has

    def tile_of(ch, which):
        tile = 0
        for k, t in TURNS[ch].items():
            tile = jnp.where(which == k, t, tile)
        return tile

    def wait_rest(ch, sem):
        count = len(TURNS[ch]) * NZ
        mine = adds_up(ch, my_class)

        @pl.when(mine)
        def _():
            wait(take.at[ch, 0, pl.ds(0, count - 1)], sem)

        @pl.when(jnp.logical_not(mine))
        def _():
            wait(take.at[ch, 0, pl.ds(0, count)], sem)

    def send_part(ch, b):
        for dy, dz in moves:
            yy, zz = lax.rem(y + dy, NY), lax.rem(z + dz, NZ)
            which = lax.rem(my_class + dy - dz + 2 * NZ, NY)

            @pl.when(adds_up(ch, which))
            def _():
                remote(
                    part.at[b, zz, tile_of(ch, which)], take.at[ch, b, dy * NZ + dz],
                    rs_send.at[ch, b], rs_recv.at[ch, b], (g, yy * NZ + zz),
                ).start()

    def add_up(ch, b):
        @pl.when(adds_up(ch, my_class))
        def _():
            wait(take.at[ch, b, pl.ds(1, 31)], rs_recv.at[ch, b])
            tile = tile_of(ch, my_class)
            total = part[b, z, tile].astype(F32)
            total += jnp.sum(take[ch, b, 1:].astype(F32), axis=0)
            coef_all[b, z, tile] = total.astype(BF16)
            ref = coef_all.at[b, z, tile]
            for dy, dz in moves:
                yy, zz = lax.rem(y + dy, NY), lax.rem(z + dz, NZ)
                remote(
                    ref, ref, ag_send.at[ch, b], ag_recv.at[ch, b], (g, yy * NZ + zz)
                ).start()

    def rows_of(ch):
        first, count = CHAINS[ch]
        return slice(16 * first, 16 * (first + count))

    def update(ch, b):
        first, count = CHAINS[ch]
        rows = rows_of(ch)
        weights = jnp.concatenate(
            [
                coef_all[b, k, first:first + count].reshape(16 * count, LANES)
                for k in range(NZ)
            ],
            axis=1,
        )
        change = jnp.dot(weights, turned[...], preferred_element_type=F32)
        remaining = chain[rows, :] - change
        chain[rows, :] = remaining
        rounded[b + 1, rows, :] = remaining.astype(BF16)
        return remaining.astype(BF16)

    def next_part(ch, b, rows):
        first, count = CHAINS[ch]
        total = jnp.dot(rows, p_all[b], preferred_element_type=F32)
        for k in range(NZ):
            part[b, k, first:first + count] = (
                total[:, k * LANES:(k + 1) * LANES].astype(BF16).reshape(count, 16, LANES)
            )

    for ch in (0, 1):
        send_part(ch, 0)

    def block_step(b, carry):
        @pl.when(b == 0)
        def _():
            pass_on(*a_way, b)

        @pl.when(b > 0)
        def _():
            pass_across(*a_way, b)

            @pl.when(b < BLOCKS - 1)
            def _():
                pass_on(*p_way, b + 1)

        for ch in (0, 1):
            add_up(ch, b)

        @pl.when(b == 0)
        def _():
            pass_across(*a_way, b)
            pass_on(*p_way, b + 1)

        @pl.when(b < BLOCKS - 1)
        def _():
            pass_across(*p_way, b + 1)
            pass_on(*a_way, b + 1)

        need_block(a_all, a_recv, b)
        turned[...] = a_all[b].T

        for ch in (0, 1):
            wait_rest(ch, ag_recv.at[ch, b])
            if ch == 1:
                @pl.when(b != g)
                def _():
                    remote(
                        coef_all.at[b], coef_in.at[g], c_send.at[b], c_recv.at[g], (b, r)
                    ).start()

            rows = update(ch, b)

            @pl.when(b < BLOCKS - 1)
            def _():
                if ch == 0:
                    need_block(p_all, p_recv, b + 1)
                next_part(ch, b + 1, rows)
                send_part(ch, b + 1)

        @pl.when(b != g)
        def _():
            remote(rounded.at[b + 1], chain_in.at[g], r_send.at[b], r_recv.at[g], (b, r)).start()

        return carry

    lax.fori_loop(0, BLOCKS, block_step, 0)

    coef_in[g] = coef_all[g]
    chain_in[g] = rounded[g + 1]

    def unpack(out, of, rows):
        rows = rows.astype(F32)
        out[PANEL * of:PANEL * of + 64, :] = rows[16:]
        out[PANEL * of + 64:PANEL * of + 72, :] = rows[:8]

    for of in range(BLOCKS):
        @pl.when(g != of)
        def _():
            wait(coef_in.at[of], c_recv.at[of])

        unpack(coef_out, of, join(coef_in[of]))

    for of in range(BLOCKS):
        @pl.when(g != of)
        def _():
            wait(chain_in.at[of], r_recv.at[of])

        unpack(sect_out, of, chain_in[of])

    @pl.when(g == 0)
    def _():
        wait(first, first_send)

    @pl.when(g > 0)
    def _():
        wait(p_all.at[pl.ds(0, 3)], own_send.at[0])

    wait(a_all.at[pl.ds(0, 3)], own_send.at[1])
    wait(a_all.at[pl.ds(0, 4)], fwd_send.at[1])

    @pl.when(jnp.logical_or(core == 1, x == 0))
    def _():
        wait(p_all.at[pl.ds(0, 4)], fwd_send.at[0])

    @pl.when(jnp.logical_and(core == 0, x == 2))
    def _():
        wait(p_all.at[pl.ds(0, 3)], fwd_send.at[0])

    @pl.when(jnp.logical_and(core == 0, lax.rem(x, 2) == 1))
    def _():
        wait(p_all.at[pl.ds(0, 5), pl.ds(0, ROWS // 2)], fwd_send.at[0])

    def drain(b, carry):
        for ch in (0, 1):
            wait_rest(ch, rs_send.at[ch, b])

            @pl.when(adds_up(ch, my_class))
            def _():
                wait(take.at[ch, b, pl.ds(1, 31)], ag_send.at[ch, b])

        @pl.when(b != g)
        def _():
            wait(coef_all.at[b], c_send.at[b])
            wait(rounded.at[b + 1], r_send.at[b])

        return carry

    lax.fori_loop(0, BLOCKS, drain, 0)


def local(features, residual, precond):
    tiles = (NZ, TILES, 16, LANES)
    sem = pltpu.SemaphoreType.DMA
    hbm = pl.BlockSpec(memory_space=pl.ANY)
    vmem = pl.BlockSpec(memory_space=pltpu.VMEM)
    coefs, section = pl.pallas_call(
        sweep_kernel,
        name="block_sweep",
        out_shape=(
            jax.ShapeDtypeStruct((TGT, BLK), F32),
            jax.ShapeDtypeStruct((TGT, ROWS), F32),
        ),
        in_specs=[hbm] * 3,
        out_specs=(vmem, vmem),
        scratch_shapes=[
            pltpu.VMEM((BLOCKS, ROWS, BLK), BF16),
            pltpu.VMEM((BLOCKS, ROWS, BLK), BF16),
            pltpu.VMEM((BLK, BLK), F32),
            pltpu.VMEM((592, ROWS), F32),
            pltpu.VMEM((WIDE, ROWS), F32),
            pltpu.VMEM((BLOCKS + 1, WIDE, ROWS), BF16),
            pltpu.VMEM((BLOCKS - 1,) + tiles, BF16),
            pltpu.VMEM((BLOCKS,) + tiles, BF16),
            pltpu.VMEM((2, BLOCKS, 32, 16, LANES), BF16),
            pltpu.VMEM((BLOCKS,) + tiles, BF16),
            pltpu.VMEM((BLOCKS,) + tiles, BF16),
            pltpu.VMEM((BLOCKS, WIDE, ROWS), BF16),
            pltpu.VMEM((BLK, ROWS), BF16),
            sem((2 + CHUNKS,)), sem, sem, sem((2,)), sem((2,)),
            sem((BLOCKS,)), sem((BLOCKS,)),
        ] + [sem((2, BLOCKS))] * 4 + [sem((BLOCKS,))] * 4,
        compiler_params=pltpu.CompilerParams(
            collective_id=0, has_side_effects=True, vmem_limit_bytes=48 * 2**20
        ),
        cost_estimate=pl.CostEstimate(
            flops=2 * 10**9, bytes_accessed=8 * 10**6, transcendentals=0
        ),
    )(features, residual.T, precond)
    return coefs.T, section.T[None]


def solution(mesh):
    placed = (P("row", "grp"), P("row", None), P("grp", None))
    return jax.shard_map(
        local,
        mesh=mesh,
        in_specs=placed,
        out_specs=(P("grp", None), P("grp", "row", None)),
        check_vma=False,
    )
```
